32 devices in a mesh: head: 8 (over y, x, core), ctx: 4 (over z).
Axes of the slice: x: 2, y: 2, z: 4, core: 2. Of those that a mesh axis runs over, the one named last changes fastest.
Arguments:
- queries: bfloat16 [16384, 2048], P(('ctx', 'head')), may hold values from -20 to 20
- key_rows: bfloat16 [16384, 2048], P(('ctx', 'head')), may hold values from -20 to 20
- value_rows: bfloat16 [16384, 2048], P(('ctx', 'head')), may hold values from -6 to 6
- band_blocks: int32 [16], P('head'), may hold values from 1 to 4, as said below
- global_list: int32 [128, 8], P('ctx'), may hold values from -1 to 119, as said below
Outputs:
- attended: bfloat16 [16384, 2048], P(('ctx', 'head'))
The draws below stay inside these ranges and needn't reach their ends.
Inputs may be any that keep to these rules, and one draw needn't show every extreme that they name: `global_list`: each entry is -1 or a key block j with j % 4 == 3 and j <= b - 5 for its row's query block b. A row's entries other than -1 are distinct and come first, the first being the largest such j, and a row holds min(8, the number of such j) of them. `band_blocks`: every value from 1 to 4 is taken by some head.
All inputs are finite; a program needn't handle non-finite values.
Results may differ from the reference program's by a relative error of at most 0.008.
Values may be sent and summed in bfloat16 or wider, within the bound.
A program may use at most 64 MiB of HBM per device.

```python
import jax
import jax.numpy as jnp
from jax import lax

HEADS = 16
HEAD_FEATURES = 128
BLOCK = 128
BAND_MAX = 4
STRIDE = 4
G = 8
SEQ = 16384
NB = 128


def draw_queries(key, part):
    key = jax.random.fold_in(key, 3)
    result = jnp.clip(jax.random.normal(key, (SEQ, HEADS * HEAD_FEATURES), jnp.float32), -6.0, 6.0)
    return result.astype(jnp.bfloat16)


def draw_key_rows(key, part):
    key = jax.random.fold_in(key, 5)
    result = jnp.clip(jax.random.normal(key, (SEQ, HEADS * HEAD_FEATURES), jnp.float32), -6.0, 6.0)
    return result.astype(jnp.bfloat16)


def draw_band_blocks(key, part):
    key = jax.random.fold_in(key, 9)
    head_order = jax.random.permutation(key, HEADS)
    return (1 + head_order % BAND_MAX).astype(jnp.int32)


def draw_global_list(key, part):
    key = jax.random.fold_in(key, 7)
    num_cand = NB // STRIDE
    query_block = jnp.arange(NB, dtype=jnp.int32)[:, None]
    candidate = jnp.arange(num_cand, dtype=jnp.int32)[None, :]
    cand_block = candidate * STRIDE + STRIDE - 1
    usable = cand_block <= query_block - BAND_MAX - 1
    latest = usable & (cand_block + STRIDE > query_block - BAND_MAX - 1)
    jitter_draw = jax.random.randint(key, (NB, num_cand), 0, 65536, jnp.int32)
    ranking = jnp.where(latest, 1 << 30, jnp.where(usable, jitter_draw * num_cand + candidate, -1 - candidate))
    best_score, picked = lax.top_k(ranking, G)
    return jnp.where(best_score >= 0, picked * STRIDE + STRIDE - 1, -1).astype(jnp.int32)


def shard_levels(own_key, extent, pieces, smallest, top_value):
    loudness = 1.0
    for position, blocks in pieces:
        steps = jax.random.uniform(jax.random.fold_in(jax.random.fold_in(own_key, 6), position), (blocks,), jnp.float32, smallest / len(pieces), top_value / len(pieces))
        loudness = loudness * jnp.repeat(jnp.exp(steps), extent[position] // blocks).reshape((-1,) + (1,) * (len(extent) - 1 - position))
    return loudness


def bell_draw(own_key, shape, scale, reach, split=(), kind=jnp.bfloat16):
    loudness = shard_levels(own_key, shape, split, -0.22, 0.18) if split else 1.0
    array = jax.random.normal(own_key, shape, jnp.float32) * scale * loudness
    return jnp.minimum(jnp.maximum(array, -reach), reach).astype(kind)


def setup_inputs(seed: int = 0) -> dict:
    key_list = jax.random.split(jax.random.key(seed), 6)
    queries = draw_queries(jax.random.fold_in(key_list[5], 71), 0)
    key_rows = draw_key_rows(jax.random.fold_in(key_list[5], 71), 0)
    value_rows = bell_draw(key_list[2], (SEQ, HEADS * HEAD_FEATURES), 1.0, 6.0, ((0, 32),))
    band_blocks = draw_band_blocks(jax.random.fold_in(key_list[5], 71), 0)
    global_list = draw_global_list(jax.random.fold_in(key_list[5], 71), 0)
    return {"queries": queries, "key_rows": key_rows, "value_rows": value_rows, "band_blocks": band_blocks, "global_list": global_list}


def band_allowed(num_blocks, reach_blocks):
    key_index = jnp.arange((BAND_MAX + 1) * BLOCK, dtype=jnp.int32)
    offset = key_index // BLOCK
    query_block = jnp.arange(num_blocks, dtype=jnp.int32)
    key_pos = (query_block[:, None] - BAND_MAX + offset[None, :]) * BLOCK + key_index[None, :] % BLOCK
    query_pos = query_block[:, None] * BLOCK + jnp.arange(BLOCK, dtype=jnp.int32)[None, :]
    causal = (key_pos[:, None, :] >= 0) & (key_pos[:, None, :] <= query_pos[:, :, None])
    return causal & (offset >= BAND_MAX - reach_blocks)[None, None, :]


def reference(queries, key_rows, value_rows, band_blocks, global_list):
    num_blocks = SEQ // BLOCK

    def split_heads(matrix):
        return matrix.reshape(num_blocks, BLOCK, HEADS, HEAD_FEATURES).transpose(2, 0, 1, 3)

    listed_ok = jnp.repeat(global_list >= 0, BLOCK, axis=1)[:, None, :]
    listed_ok = jnp.broadcast_to(listed_ok, (num_blocks, BLOCK, G * BLOCK))
    picked_blocks = jnp.maximum(global_list, 0).astype(jnp.int32)

    def one_head(operands):
        head_query_rows, key_head, value_head, reach_blocks = operands
        zero_pad = jnp.zeros((BAND_MAX, BLOCK, HEAD_FEATURES), key_head.dtype)
        key_padded = jnp.concatenate([zero_pad, key_head], axis=0)
        value_padded = jnp.concatenate([zero_pad, value_head], axis=0)
        key_band = jnp.stack([key_padded[offset:offset + num_blocks] for offset in range(BAND_MAX + 1)], axis=1)
        value_band = jnp.stack([value_padded[offset:offset + num_blocks] for offset in range(BAND_MAX + 1)], axis=1)
        key_band = key_band.reshape(num_blocks, (BAND_MAX + 1) * BLOCK, HEAD_FEATURES)
        value_band = value_band.reshape(num_blocks, (BAND_MAX + 1) * BLOCK, HEAD_FEATURES)
        key_global = key_head[picked_blocks].reshape(num_blocks, G * BLOCK, HEAD_FEATURES)
        value_global = value_head[picked_blocks].reshape(num_blocks, G * BLOCK, HEAD_FEATURES)
        every_key_row = jnp.concatenate([key_band, key_global], axis=1).astype(jnp.float32)
        every_value_row = jnp.concatenate([value_band, value_global], axis=1).astype(jnp.float32)
        logit_matrix = jnp.einsum("tvi,tui->tvu", head_query_rows.astype(jnp.float32), every_key_row) * (HEAD_FEATURES ** -0.5)
        allowed = jnp.concatenate([band_allowed(num_blocks, reach_blocks), listed_ok], axis=-1)
        row_top = jnp.max(jnp.where(allowed, logit_matrix, -1e30), axis=-1, keepdims=True)
        weights_raw = jnp.where(allowed, jnp.exp(logit_matrix - row_top), 0.0)
        row_weight_sum = jnp.sum(weights_raw, axis=-1, keepdims=True)
        attention_probs = lax.optimization_barrier(weights_raw.astype(jnp.bfloat16)).astype(jnp.float32)
        blended_output = jnp.einsum("atg,agh->ath", attention_probs, every_value_row) / row_weight_sum
        return blended_output.astype(jnp.bfloat16)

    heads_out = lax.map(one_head, (split_heads(queries), split_heads(key_rows), split_heads(value_rows), band_blocks))
    return heads_out.transpose(1, 2, 0, 3).reshape(SEQ, HEADS * HEAD_FEATURES)
```

```python
import functools
import math

import jax
import jax.numpy as jnp
from jax import lax
from jax.experimental import pallas as pl
from jax.experimental.pallas import tpu as pltpu
from jax.sharding import PartitionSpec as P

D = 128
BLOCK = 128
BAND = 4
G = 8
NEG = -1e30
SCALE2 = D ** (-0.5) * math.log2(math.e)


def kernel(
    heads, ctxs, rows, feat,
    band_ref, list_ref, q_hbm, k_hbm, v_hbm, out_ref,
    q, k, v, kc, vc, o,
    send, recv, chain_send, chain_recv, rim_send, rim_recv, fill_sem,
):
    me = lax.axis_index("head")
    z = lax.axis_index("ctx")
    per = rows // BLOCK
    rim = BAND * BLOCK
    length = heads * rows
    rest = rows - BLOCK
    hpd = feat // D

    barrier = pltpu.get_barrier_semaphore()

    @pl.loop(1, heads)
    def _(delta):
        pl.semaphore_signal(barrier, inc=1, device_id={"head": (me + delta) % heads})

    pl.semaphore_signal(barrier, inc=1, device_id={"ctx": (z + 1) % ctxs})
    pl.semaphore_signal(barrier, inc=1, device_id={"ctx": (z + ctxs - 1) % ctxs})
    pl.semaphore_wait(barrier, heads + 1)

    def col(p):
        return pl.ds(pl.multiple_of(p * feat, 128), feat)

    def row(s, first, n):
        return pl.ds(pl.multiple_of(first + s * rows, 128), n)

    def src(kind, p):
        if kind == 0:
            return k_hbm.at[pl.ds(rest, BLOCK), col(p)]
        if kind == 1:
            return v_hbm.at[pl.ds(rest, BLOCK), col(p)]
        if kind == 2:
            return k_hbm.at[pl.ds(0, rest), col(p)]
        if kind == 3:
            return v_hbm.at[pl.ds(0, rest), col(p)]
        return q_hbm.at[:, col(p)]

    def dst(kind, s):
        if kind == 0:
            return kc.at[z * heads + s]
        if kind == 1:
            return vc.at[z * heads + s]
        if kind == 2:
            return k.at[row(s, rim, rest), :]
        if kind == 3:
            return v.at[row(s, rim, rest), :]
        return q.at[row(s, 0, rows), :]

    def outgoing(kind, delta):
        return pltpu.make_async_remote_copy(
            src_ref=src(kind, (me + delta) % heads),
            dst_ref=dst(kind, me),
            send_sem=send.at[kind, delta],
            recv_sem=recv.at[kind, delta],
            device_id={"head": (me + delta) % heads},
        )

    def incoming(kind, delta):
        s = (me + heads - delta) % heads
        return pltpu.make_async_remote_copy(
            src_ref=src(kind, s),
            dst_ref=dst(kind, s),
            send_sem=send.at[kind, delta],
            recv_sem=recv.at[kind, delta],
            device_id={"head": s},
        )

    def own(kind):
        return pltpu.make_async_copy(src(kind, me), dst(kind, me), send.at[kind, 0])

    def start(kind):
        @pl.loop(1, heads)
        def _(delta):
            outgoing(kind, delta).start()

        own(kind).start()

    def arrive(kind):
        @pl.loop(1, heads)
        def _(delta):
            incoming(kind, delta).wait_recv()

        own(kind).wait()

    def sent(kind):
        @pl.loop(1, heads)
        def _(delta):
            outgoing(kind, delta).wait_send()

    def fill(which, s):
        big, cand = (k, kc) if which == 0 else (v, vc)
        return pltpu.make_async_copy(
            cand.at[z * heads + s], big.at[row(s, rim + rest, BLOCK), :], fill_sem.at[which, s]
        )

    def chain(which, t, group):
        buf = kc if which == 0 else vc
        part = buf.at[pl.ds(group * heads, heads)]
        return pltpu.make_async_remote_copy(
            src_ref=part,
            dst_ref=part,
            send_sem=chain_send.at[which, t],
            recv_sem=chain_recv.at[which, t],
            device_id={"ctx": (z + 1) % ctxs},
        )

    def edge(which):
        big = k if which == 0 else v
        return pltpu.make_async_remote_copy(
            src_ref=big.at[pl.ds(length, rim), :],
            dst_ref=big.at[pl.ds(0, rim), :],
            send_sem=rim_send.at[which],
            recv_sem=rim_recv.at[which],
            device_id={"ctx": (z + 1) % ctxs},
        )

    start(0)
    start(1)
    if rest:
        start(2)

    @pl.when(z == 0)
    def _():
        k[pl.ds(0, rim), :] = jnp.zeros((rim, feat), k.dtype)
        v[pl.ds(0, rim), :] = jnp.zeros((rim, feat), v.dtype)

    arrive(0)
    arrive(1)

    @pl.when(z + 1 < ctxs)
    def _():
        chain(0, 0, z).start()
        chain(1, 0, z).start()

    @pl.loop(0, heads)
    def _(s):
        fill(0, s).start()
        fill(1, s).start()

    if rest:
        start(3)
    start(4)

    @pl.loop(0, heads)
    def _(s):
        fill(0, s).wait()
        fill(1, s).wait()

    if rest:
        arrive(2)
        arrive(3)

    @pl.when(z + 1 < ctxs)
    def _():
        edge(0).start()
        edge(1).start()

    @pl.loop(0, ctxs - 1)
    def _(t):
        @pl.when((t > 0) & (z + 1 < ctxs) & (z >= t))
        def _():
            chain(0, t, z - t).start()
            chain(1, t, z - t).start()

        @pl.when(z >= t + 1)
        def _():
            chain(0, t, z - 1 - t).wait_recv()
            chain(1, t, z - 1 - t).wait_recv()

    @pl.when(z > 0)
    def _():
        edge(0).wait_recv()
        edge(1).wait_recv()

    arrive(4)

    tri = lax.broadcasted_iota(jnp.int32, (BLOCK, BLOCK), 1) <= lax.broadcasted_iota(
        jnp.int32, (BLOCK, BLOCK), 0
    )
    first = z * (length // BLOCK)

    def attend(b, h):
        hs = pl.ds(h * D, D)
        base = pl.multiple_of(b * BLOCK, 128)
        qb = q[pl.ds(base, BLOCK), hs]
        window = pl.ds(base, (BAND + 1) * BLOCK)
        listed = [list_ref[b, g] for g in range(G)]
        slots = [jnp.maximum(j, 0) // per for j in listed]
        keys = jnp.concatenate([k[window, hs]] + [kc[i, :, hs] for i in slots], axis=0)
        values = jnp.concatenate([v[window, hs]] + [vc[i, :, hs] for i in slots], axis=0)
        s = lax.dot_general(
            qb, keys, (((1,), (1,)), ((), ())), preferred_element_type=jnp.float32
        )
        parts = [s[:, i * BLOCK : (i + 1) * BLOCK] for i in range(BAND + 1 + G)]
        parts[BAND] = jnp.where(tri, parts[BAND], NEG)
        reach = band_ref[h]
        bias = [
            jnp.where((reach >= BAND - i) & (first + b >= BAND - i), 0.0, NEG) for i in range(BAND)
        ]
        bias = bias + [None] + [jnp.where(j >= 0, 0.0, NEG) for j in listed]
        top = parts[BAND]
        for part, off in zip(parts, bias):
            if off is not None:
                top = jnp.maximum(top, part + off)
        top = jnp.max(top, axis=1, keepdims=True) * SCALE2
        weights = []
        for part, off in zip(parts, bias):
            shift = top if off is None else top - off
            weights.append(jnp.exp2(part * SCALE2 - shift))
        total = functools.reduce(jnp.add, weights)
        total = jnp.sum(total, axis=1, keepdims=True)
        w = jnp.concatenate([x.astype(jnp.bfloat16) for x in weights], axis=1)
        acc = jnp.dot(w, values, preferred_element_type=jnp.float32)
        o[pl.ds(base, BLOCK), hs] = (acc / total).astype(o.dtype)

    def give(delta):
        p = (me + delta) % heads
        return pltpu.make_async_remote_copy(
            src_ref=o.at[row(p, 0, rows), :],
            dst_ref=out_ref.at[:, col(me)],
            send_sem=send.at[5, delta],
            recv_sem=recv.at[5, delta],
            device_id={"head": p},
        )

    def take(delta):
        p = (me + heads - delta) % heads
        return pltpu.make_async_remote_copy(
            src_ref=o.at[row(p, 0, rows), :],
            dst_ref=out_ref.at[:, col(p)],
            send_sem=send.at[5, delta],
            recv_sem=recv.at[5, delta],
            device_id={"head": p},
        )

    def group(delta):
        @pl.loop(0, per)
        def _(j):
            for h in range(hpd):
                attend((me + delta) % heads * per + j, h)

    @pl.loop(1, heads)
    def _(delta):
        group(delta)
        give(delta).start()

    group(0)
    mine = pltpu.make_async_copy(o.at[row(me, 0, rows), :], out_ref.at[:, col(me)], send.at[5, 0])
    mine.start()

    for kind in range(5):
        if rest or kind not in (2, 3):
            sent(kind)

    @pl.when(z + 1 < ctxs)
    def _():
        edge(0).wait_send()
        edge(1).wait_send()

    @pl.loop(0, ctxs - 1)
    def _(t):
        @pl.when((z + 1 < ctxs) & (z >= t))
        def _():
            chain(0, t, z - t).wait_send()
            chain(1, t, z - t).wait_send()

    @pl.loop(1, heads)
    def _(delta):
        give(delta).wait_send()
        take(delta).wait_recv()

    mine.wait()


def solution(mesh):
    heads, ctxs = mesh.shape["head"], mesh.shape["ctx"]

    def local(queries, key_rows, value_rows, band_blocks, global_list):
        rows, width = queries.shape
        feat = width // heads
        length = rows * heads
        rim = BAND * BLOCK
        assert rows % BLOCK == 0 and BAND % (rows // BLOCK) == 0
        bf = jnp.bfloat16
        dma = pltpu.SemaphoreType.DMA
        return pl.pallas_call(
            functools.partial(kernel, heads, ctxs, rows, feat),
            out_shape=jax.ShapeDtypeStruct((rows, width), bf),
            in_specs=[pl.BlockSpec(memory_space=pltpu.SMEM)] * 2
            + [pl.BlockSpec(memory_space=pl.ANY)] * 3,
            out_specs=pl.BlockSpec(memory_space=pl.ANY),
            scratch_shapes=[
                pltpu.VMEM((length, feat), bf),
                pltpu.VMEM((length + rim, feat), bf),
                pltpu.VMEM((length + rim, feat), bf),
                pltpu.VMEM((ctxs * heads, BLOCK, feat), bf),
                pltpu.VMEM((ctxs * heads, BLOCK, feat), bf),
                pltpu.VMEM((length, feat), bf),
                dma((6, heads)),
                dma((6, heads)),
                dma((2, ctxs)),
                dma((2, ctxs)),
                dma((2,)),
                dma((2,)),
                dma((2, heads)),
            ],
            compiler_params=pltpu.CompilerParams(
                collective_id=0, has_side_effects=True, vmem_limit_bytes=48 * 1024 * 1024
            ),
        )(band_blocks, global_list, queries, key_rows, value_rows)

    in_specs = (
        P(("ctx", "head"), None),
        P(("ctx", "head"), None),
        P(("ctx", "head"), None),
        P("head"),
        P("ctx", None),
    )
    return jax.shard_map(
        local, mesh=mesh, in_specs=in_specs, out_specs=P(("ctx", "head"), None), check_vma=False
    )
```

```python
import functools
import math

import jax
import jax.numpy as jnp
from jax import lax
from jax.experimental import pallas as pl
from jax.experimental.pallas import tpu as pltpu
from jax.sharding import PartitionSpec as P

D = 128
BLOCK = 128
BAND = 4
G = 8
NEG = -1e30
SCALE2 = D ** (-0.5) * math.log2(math.e)


def kernel(
    heads, ctxs, rows, feat,
    band_ref, list_ref, q_hbm, k_hbm, v_hbm, out_ref,
    q, k, v, kc, vc, o, acc, top, total,
    send, recv, give_send, give_recv, chain_send, chain_recv, rim_send, rim_recv, fill_sem,
):
    me = lax.axis_index("head")
    z = lax.axis_index("ctx")
    per = rows // BLOCK
    rim = BAND * BLOCK
    length = heads * rows
    rest = rows - BLOCK
    hpd = feat // D

    barrier = pltpu.get_barrier_semaphore()

    @pl.loop(1, heads)
    def _(delta):
        pl.semaphore_signal(barrier, inc=1, device_id={"head": (me + delta) % heads})

    pl.semaphore_signal(barrier, inc=1, device_id={"ctx": (z + 1) % ctxs})
    pl.semaphore_signal(barrier, inc=1, device_id={"ctx": (z + ctxs - 1) % ctxs})
    pl.semaphore_wait(barrier, heads + 1)

    def col(p):
        return pl.ds(pl.multiple_of(p * feat, 128), feat)

    def row(s, first, n):
        return pl.ds(pl.multiple_of(first + s * rows, 128), n)

    k_rest, v_rest, q_all = 2 * hpd, 2 * hpd + 1, 2 * hpd + 2

    def last(which, h):
        return 2 * h + which

    def src(kind, p):
        if kind < k_rest:
            hbm = v_hbm if kind % 2 else k_hbm
            at = pl.multiple_of(p * feat + kind // 2 * D, 128)
            return hbm.at[pl.ds(rest, BLOCK), pl.ds(at, D)]
        if kind == k_rest:
            return k_hbm.at[pl.ds(0, rest), col(p)]
        if kind == v_rest:
            return v_hbm.at[pl.ds(0, rest), col(p)]
        return q_hbm.at[:, col(p)]

    def dst(kind, s):
        if kind < k_rest:
            return (vc if kind % 2 else kc)[kind // 2].at[z * heads + s]
        if kind == k_rest:
            return k.at[row(s, rim, rest), :]
        if kind == v_rest:
            return v.at[row(s, rim, rest), :]
        return q.at[row(s, 0, rows), :]

    def outgoing(kind, delta):
        return pltpu.make_async_remote_copy(
            src_ref=src(kind, (me + delta) % heads),
            dst_ref=dst(kind, me),
            send_sem=send.at[kind, delta],
            recv_sem=recv.at[kind, delta],
            device_id={"head": (me + delta) % heads},
        )

    def incoming(kind, delta):
        s = (me + heads - delta) % heads
        return pltpu.make_async_remote_copy(
            src_ref=src(kind, s),
            dst_ref=dst(kind, s),
            send_sem=send.at[kind, delta],
            recv_sem=recv.at[kind, delta],
            device_id={"head": s},
        )

    def own(kind):
        return pltpu.make_async_copy(src(kind, me), dst(kind, me), send.at[kind, 0])

    def start(kind):
        @pl.loop(1, heads)
        def _(delta):
            outgoing(kind, delta).start()

        own(kind).start()

    def arrive(kind):
        @pl.loop(1, heads)
        def _(delta):
            incoming(kind, delta).wait_recv()

        own(kind).wait()

    def sent(kind):
        @pl.loop(1, heads)
        def _(delta):
            outgoing(kind, delta).wait_send()

    def fill(which, s, h):
        big, cand = (k, kc) if which == 0 else (v, vc)
        return pltpu.make_async_copy(
            cand[h].at[z * heads + s],
            big.at[row(s, rim + rest, BLOCK), pl.ds(h * D, D)],
            fill_sem.at[which, s, h],
        )

    def chain(which, t, group, s, h):
        part = (kc if which == 0 else vc)[h].at[group * heads + s]
        return pltpu.make_async_remote_copy(
            src_ref=part,
            dst_ref=part,
            send_sem=chain_send.at[which, t, s, h],
            recv_sem=chain_recv.at[which, t, s, h],
            device_id={"ctx": (z + 1) % ctxs},
        )

    def edge(which):
        big = k if which == 0 else v
        return pltpu.make_async_remote_copy(
            src_ref=big.at[pl.ds(length, rim), :],
            dst_ref=big.at[pl.ds(0, rim), :],
            send_sem=rim_send.at[which],
            recv_sem=rim_recv.at[which],
            device_id={"ctx": (z + 1) % ctxs},
        )

    for kind in range(k_rest):
        start(kind)
    if rest:
        start(k_rest)

    @pl.when(z == 0)
    def _():
        k[pl.ds(0, rim), :] = jnp.zeros((rim, feat), k.dtype)
        v[pl.ds(0, rim), :] = jnp.zeros((rim, feat), v.dtype)

    if rest:
        start(v_rest)
    start(q_all)

    def pass_on(s, h):
        @pl.when(z + 1 < ctxs)
        def _():
            chain(0, 0, z, s, h).start()
            chain(1, 0, z, s, h).start()

        fill(0, s, h).start()
        fill(1, s, h).start()

    def forward(t, s, h):
        for which in range(2):
            chain(which, t - 1, z - t, s, h).wait_recv()
            chain(which, t, z - t, s, h).start()

    def forward_all(t, h):
        @pl.when((z + 1 < ctxs) & (z >= t))
        def _():
            @pl.loop(0, heads)
            def _(delta):
                forward(t, (me + heads - delta) % heads, h)

    for h in range(hpd):
        own(last(0, h)).wait()
        own(last(1, h)).wait()
        pass_on(me, h)

        @pl.loop(1, heads)
        def _(delta):
            incoming(last(0, h), delta).wait_recv()
            incoming(last(1, h), delta).wait_recv()
            pass_on((me + heads - delta) % heads, h)

        if h == 0:

            @pl.loop(1, ctxs - 1)
            def _(t):
                forward_all(t, 0)

    @pl.loop(0, heads)
    def _(s):
        for h in range(hpd):
            fill(0, s, h).wait()
            fill(1, s, h).wait()

    if rest:
        arrive(k_rest)
        arrive(v_rest)

    @pl.when(z + 1 < ctxs)
    def _():
        edge(0).start()
        edge(1).start()

    for h in range(1, hpd):
        forward_all(1, h)

    tri = lax.broadcasted_iota(jnp.int32, (BLOCK, BLOCK), 1) <= lax.broadcasted_iota(
        jnp.int32, (BLOCK, BLOCK), 0
    )
    first = z * (length // BLOCK)

    def weigh(parts, bias, peak):
        weights = []
        for part, off in zip(parts, bias):
            shift = peak if off is None else peak - off
            weights.append(jnp.exp2(part * SCALE2 - shift))
        added = jnp.sum(functools.reduce(jnp.add, weights), axis=1, keepdims=True)
        return jnp.concatenate([x.astype(jnp.bfloat16) for x in weights], axis=1), added

    def scores(qb, keys):
        s = lax.dot_general(
            qb, keys, (((1,), (1,)), ((), ())), preferred_element_type=jnp.float32
        )
        return [s[:, i : i + BLOCK] for i in range(0, s.shape[1], BLOCK)]

    def place(b, h):
        return pl.ds(pl.multiple_of(b * BLOCK, 128), BLOCK), pl.ds(h * D, D)

    def near(b, h):
        at = place(b, h)
        window = pl.ds(pl.multiple_of(b * BLOCK, 128), (BAND + 1) * BLOCK)
        parts = scores(q[at], k[window, at[1]])
        parts[BAND] = jnp.where(tri, parts[BAND], NEG)
        reach = band_ref[h]
        bias = [
            jnp.where((reach >= BAND - i) & (first + b >= BAND - i), 0.0, NEG) for i in range(BAND)
        ]
        peak = parts[BAND]
        for part, off in zip(parts, bias):
            peak = jnp.maximum(peak, part + off)
        peak = jnp.max(peak, axis=1, keepdims=True) * SCALE2
        w, added = weigh(parts, bias + [None], peak)
        acc[at] = jnp.dot(w, v[window, at[1]], preferred_element_type=jnp.float32)
        top[at] = jnp.broadcast_to(peak, (BLOCK, D))
        total[at] = jnp.broadcast_to(added, (BLOCK, D))

    def far(b, h):
        at = place(b, h)
        listed = [list_ref[b, g] for g in range(G)]
        slots = [jnp.maximum(j, 0) // per for j in listed]
        keys = jnp.concatenate([kc[h][i] for i in slots], axis=0)
        values = jnp.concatenate([vc[h][i] for i in slots], axis=0)
        parts = scores(q[at], keys)
        bias = [jnp.where(j >= 0, 0.0, NEG) for j in listed]
        peak = functools.reduce(jnp.maximum, [part + off for part, off in zip(parts, bias)])
        before = top[at]
        peak = jnp.maximum(before, jnp.max(peak, axis=1, keepdims=True) * SCALE2)
        w, added = weigh(parts, bias, peak)
        keep = jnp.exp2(before - peak)
        blend = acc[at] * keep + jnp.dot(w, values, preferred_element_type=jnp.float32)
        o[at] = (blend / (total[at] * keep + added)).astype(o.dtype)

    def give(delta, h):
        p = (me + delta) % heads
        return pltpu.make_async_remote_copy(
            src_ref=o.at[row(p, 0, rows), pl.ds(h * D, D)],
            dst_ref=out_ref.at[:, pl.ds(pl.multiple_of(me * feat + h * D, 128), D)],
            send_sem=give_send.at[h, delta],
            recv_sem=give_recv.at[h, delta],
            device_id={"head": p},
        )

    def take(delta, h):
        p = (me + heads - delta) % heads
        return pltpu.make_async_remote_copy(
            src_ref=o.at[row(p, 0, rows), pl.ds(h * D, D)],
            dst_ref=out_ref.at[:, pl.ds(pl.multiple_of(p * feat + h * D, 128), D)],
            send_sem=give_send.at[h, delta],
            recv_sem=give_recv.at[h, delta],
            device_id={"head": p},
        )

    def mine(h):
        return pltpu.make_async_copy(
            o.at[row(me, 0, rows), pl.ds(h * D, D)],
            out_ref.at[:, pl.ds(pl.multiple_of(me * feat + h * D, 128), D)],
            give_send.at[h, 0],
        )

    def near_group(s):
        @pl.loop(0, per)
        def _(j):
            for h in range(hpd):
                near(s * per + j, h)

    def finish(s, delta, h):
        pair = math.gcd(per, 2)

        @pl.loop(0, per // pair)
        def _(j):
            for i in range(pair):
                far(s * per + j * pair + i, h)

        @pl.when(delta == 0)
        def _():
            mine(h).start()

        @pl.when(delta > 0)
        def _():
            give(delta, h).start()

    inner = rim // rows

    @pl.loop(0, heads)
    def _(delta):
        s = (me + heads - delta) % heads

        @pl.when(delta == 0)
        def _():
            own(q_all).wait()

        @pl.when(delta > 0)
        def _():
            incoming(q_all, delta).wait_recv()

        @pl.when(s >= inner)
        def _():
            near_group(s)

        for h in range(1, hpd):

            @pl.loop(2, ctxs - 1)
            def _(t):
                @pl.when((z + 1 < ctxs) & (z >= t))
                def _():
                    forward(t, s, h)

    for h in range(hpd):

        @pl.when(z + 1 == ctxs)
        def _():
            @pl.loop(0, ctxs - 1)
            def _(t):
                @pl.loop(0, heads)
                def _(s):
                    chain(0, t, z - 1 - t, s, h).wait_recv()
                    chain(1, t, z - 1 - t, s, h).wait_recv()

        if h == 0:

            @pl.loop(1, heads + 1)
            def _(step):
                delta = step % heads
                s = (me + delta) % heads

                @pl.when(s >= inner)
                def _():
                    finish(s, delta, h)

            @pl.when(z > 0)
            def _():
                edge(0).wait_recv()
                edge(1).wait_recv()

            @pl.loop(0, inner)
            def _(s):
                near_group(s)
                finish(s, (s + heads - me) % heads, h)
        else:

            @pl.loop(1, heads + 1)
            def _(step):
                delta = step % heads
                finish((me + delta) % heads, delta, h)

    for kind in range(q_all + 1):
        if rest or kind not in (k_rest, v_rest):
            sent(kind)

    @pl.when(z + 1 < ctxs)
    def _():
        edge(0).wait_send()
        edge(1).wait_send()

    @pl.loop(0, ctxs - 1)
    def _(t):
        @pl.when((z + 1 < ctxs) & (z >= t))
        def _():
            @pl.loop(0, heads)
            def _(s):
                for h in range(hpd):
                    chain(0, t, z - t, s, h).wait_send()
                    chain(1, t, z - t, s, h).wait_send()

    @pl.loop(1, heads)
    def _(delta):
        for h in range(hpd):
            give(delta, h).wait_send()
            take(delta, h).wait_recv()

    for h in range(hpd):
        mine(h).wait()


def solution(mesh):
    heads, ctxs = mesh.shape["head"], mesh.shape["ctx"]

    def local(queries, key_rows, value_rows, band_blocks, global_list):
        rows, width = queries.shape
        feat = width // heads
        length = rows * heads
        rim = BAND * BLOCK
        assert rows % BLOCK == 0 and BAND % (rows // BLOCK) == 0
        bf = jnp.bfloat16
        dma = pltpu.SemaphoreType.DMA
        return pl.pallas_call(
            functools.partial(kernel, heads, ctxs, rows, feat),
            out_shape=jax.ShapeDtypeStruct((rows, width), bf),
            in_specs=[pl.BlockSpec(memory_space=pltpu.SMEM)] * 2
            + [pl.BlockSpec(memory_space=pl.ANY)] * 3,
            out_specs=pl.BlockSpec(memory_space=pl.ANY),
            scratch_shapes=[
                pltpu.VMEM((length, feat), bf),
                pltpu.VMEM((length + rim, feat), bf),
                pltpu.VMEM((length + rim, feat), bf),
                [pltpu.VMEM((ctxs * heads, BLOCK, D), bf) for _ in range(feat // D)],
                [pltpu.VMEM((ctxs * heads, BLOCK, D), bf) for _ in range(feat // D)],
                pltpu.VMEM((length, feat), bf),
                pltpu.VMEM((length, feat), jnp.float32),
                pltpu.VMEM((length, feat), jnp.float32),
                pltpu.VMEM((length, feat), jnp.float32),
                dma((2 * (feat // D) + 3, heads)),
                dma((2 * (feat // D) + 3, heads)),
                dma((feat // D, heads)),
                dma((feat // D, heads)),
                dma((2, ctxs, heads, feat // D)),
                dma((2, ctxs, heads, feat // D)),
                dma((2,)),
                dma((2,)),
                dma((2, heads, feat // D)),
            ],
            compiler_params=pltpu.CompilerParams(
                collective_id=0, has_side_effects=True, vmem_limit_bytes=48 * 1024 * 1024
            ),
        )(band_blocks, global_list, queries, key_rows, value_rows)

    in_specs = (
        P(("ctx", "head"), None),
        P(("ctx", "head"), None),
        P(("ctx", "head"), None),
        P("head"),
        P("ctx", None),
    )
    return jax.shard_map(
        local, mesh=mesh, in_specs=in_specs, out_specs=P(("ctx", "head"), None), check_vma=False
    )
```

```python
import functools
import math

import jax
import jax.numpy as jnp
from jax import lax
from jax.experimental import pallas as pl
from jax.experimental.pallas import tpu as pltpu
from jax.sharding import PartitionSpec as P

D = 128
BLOCK = 128
BAND = 4
G = 8
NEG = -1e30
SCALE2 = D ** (-0.5) * math.log2(math.e)


def kernel(
    heads, ctxs, rows, feat,
    band_ref, list_ref, q_hbm, k_hbm, v_hbm, out_ref,
    q, k, v, kc, vc, o, acc, top, total,
    send, recv, give_send, give_recv, chain_send, chain_recv, rim_send, rim_recv, fill_sem,
):
    me = lax.axis_index("head")
    z = lax.axis_index("ctx")
    per = rows // BLOCK
    rim = BAND * BLOCK
    length = heads * rows
    rest = rows - BLOCK
    hpd = feat // D

    barrier = pltpu.get_barrier_semaphore()

    @pl.loop(1, heads)
    def _(delta):
        pl.semaphore_signal(barrier, inc=1, device_id={"head": (me + delta) % heads})

    pl.semaphore_signal(barrier, inc=1, device_id={"ctx": (z + 1) % ctxs})
    pl.semaphore_signal(barrier, inc=1, device_id={"ctx": (z + ctxs - 1) % ctxs})
    pl.semaphore_wait(barrier, heads + 1)

    def col(p):
        return pl.ds(pl.multiple_of(p * feat, 128), feat)

    def row(s, first, n):
        return pl.ds(pl.multiple_of(first + s * rows, 128), n)

    def last(which, h):
        return 2 * h + which

    def before(which, h):
        return 2 * hpd + 2 * h + which

    def query(h):
        return 4 * hpd + h

    kinds = range(5 * hpd)

    def src(kind, p):
        if kind >= 4 * hpd:
            hbm, h, at = q_hbm, kind - 4 * hpd, pl.ds(0, rows)
        else:
            hbm, h = (v_hbm if kind % 2 else k_hbm), kind // 2 % hpd
            at = pl.ds(rest, BLOCK) if kind < 2 * hpd else pl.ds(0, rest)
        return hbm.at[at, pl.ds(pl.multiple_of(p * feat + h * D, 128), D)]

    def dst(kind, s):
        if kind >= 4 * hpd:
            return q.at[row(s, 0, rows), pl.ds((kind - 4 * hpd) * D, D)]
        if kind < 2 * hpd:
            return (vc if kind % 2 else kc)[kind // 2].at[z * heads + s]
        return (v if kind % 2 else k).at[row(s, rim, rest), pl.ds(kind // 2 % hpd * D, D)]

    def outgoing(kind, delta):
        return pltpu.make_async_remote_copy(
            src_ref=src(kind, (me + delta) % heads),
            dst_ref=dst(kind, me),
            send_sem=send.at[kind, delta],
            recv_sem=recv.at[kind, delta],
            device_id={"head": (me + delta) % heads},
        )

    def incoming(kind, delta):
        s = (me + heads - delta) % heads
        return pltpu.make_async_remote_copy(
            src_ref=src(kind, s),
            dst_ref=dst(kind, s),
            send_sem=send.at[kind, delta],
            recv_sem=recv.at[kind, delta],
            device_id={"head": s},
        )

    def own(kind):
        return pltpu.make_async_copy(src(kind, me), dst(kind, me), send.at[kind, 0])

    def start(kind):
        @pl.loop(1, heads)
        def _(delta):
            outgoing(kind, delta).start()

        own(kind).start()

    def arrive(kind):
        @pl.loop(1, heads)
        def _(delta):
            incoming(kind, delta).wait_recv()

        own(kind).wait()

    def sent(kind):
        @pl.loop(1, heads)
        def _(delta):
            outgoing(kind, delta).wait_send()

    def fill(which, s, h):
        big, cand = (k, kc) if which == 0 else (v, vc)
        return pltpu.make_async_copy(
            cand[h].at[z * heads + s],
            big.at[row(s, rim + rest, BLOCK), pl.ds(h * D, D)],
            fill_sem.at[which, s, h],
        )

    def chain(which, t, group, s, h):
        part = (kc if which == 0 else vc)[h].at[group * heads + s]
        return pltpu.make_async_remote_copy(
            src_ref=part,
            dst_ref=part,
            send_sem=chain_send.at[which, t, s, h],
            recv_sem=chain_recv.at[which, t, s, h],
            device_id={"ctx": (z + 1) % ctxs},
        )

    def edge(which, h):
        big = k if which == 0 else v
        hs = pl.ds(h * D, D)
        return pltpu.make_async_remote_copy(
            src_ref=big.at[pl.ds(length, rim), hs],
            dst_ref=big.at[pl.ds(0, rim), hs],
            send_sem=rim_send.at[which, h],
            recv_sem=rim_recv.at[which, h],
            device_id={"ctx": (z + 1) % ctxs},
        )

    def start_head(h):
        if rest:
            start(before(0, h))
            start(before(1, h))
        start(query(h))

    for kind in range(2 * hpd):
        start(kind)
    start_head(0)

    @pl.when(z == 0)
    def _():
        k[pl.ds(0, rim), :] = jnp.zeros((rim, feat), k.dtype)
        v[pl.ds(0, rim), :] = jnp.zeros((rim, feat), v.dtype)

    def pass_on(s, h):
        @pl.when(z + 1 < ctxs)
        def _():
            chain(0, 0, z, s, h).start()
            chain(1, 0, z, s, h).start()

        fill(0, s, h).start()
        fill(1, s, h).start()

    def forward(t, s, h):
        for which in range(2):
            chain(which, t - 1, z - t, s, h).wait_recv()
            chain(which, t, z - t, s, h).start()

    def forward_all(t, h):
        @pl.when((z + 1 < ctxs) & (z >= t))
        def _():
            @pl.loop(0, heads)
            def _(delta):
                forward(t, (me + heads - delta) % heads, h)

    for h in range(hpd):
        own(last(0, h)).wait()
        own(last(1, h)).wait()
        pass_on(me, h)

        @pl.loop(1, heads)
        def _(delta):
            incoming(last(0, h), delta).wait_recv()
            incoming(last(1, h), delta).wait_recv()
            pass_on((me + heads - delta) % heads, h)

        if h == 0:

            @pl.loop(1, ctxs - 1)
            def _(t):
                forward_all(t, 0)

    @pl.loop(0, heads)
    def _(s):
        for h in range(hpd):
            fill(0, s, h).wait()
            fill(1, s, h).wait()

    def keys_here(h):
        if rest:
            arrive(before(0, h))
            arrive(before(1, h))
        if h + 1 < hpd:
            start_head(h + 1)

        @pl.when(z + 1 < ctxs)
        def _():
            edge(0, h).start()
            edge(1, h).start()

    keys_here(0)
    for h in range(1, hpd):
        forward_all(1, h)

    tri = lax.broadcasted_iota(jnp.int32, (BLOCK, BLOCK), 1) <= lax.broadcasted_iota(
        jnp.int32, (BLOCK, BLOCK), 0
    )
    first = z * (length // BLOCK)

    def weigh(parts, bias, peak):
        weights = []
        for part, off in zip(parts, bias):
            shift = peak if off is None else peak - off
            weights.append(jnp.exp2(part * SCALE2 - shift))
        added = jnp.sum(functools.reduce(jnp.add, weights), axis=1, keepdims=True)
        return jnp.concatenate([x.astype(jnp.bfloat16) for x in weights], axis=1), added

    def scores(qb, keys):
        s = lax.dot_general(
            qb, keys, (((1,), (1,)), ((), ())), preferred_element_type=jnp.float32
        )
        return [s[:, i : i + BLOCK] for i in range(0, s.shape[1], BLOCK)]

    def place(b, h):
        return pl.ds(pl.multiple_of(b * BLOCK, 128), BLOCK), pl.ds(h * D, D)

    def near(b, h):
        at = place(b, h)
        window = pl.ds(pl.multiple_of(b * BLOCK, 128), (BAND + 1) * BLOCK)
        parts = scores(q[at], k[window, at[1]])
        parts[BAND] = jnp.where(tri, parts[BAND], NEG)
        reach = band_ref[h]
        bias = [
            jnp.where((reach >= BAND - i) & (first + b >= BAND - i), 0.0, NEG) for i in range(BAND)
        ]
        peak = parts[BAND]
        for part, off in zip(parts, bias):
            peak = jnp.maximum(peak, part + off)
        peak = jnp.max(peak, axis=1, keepdims=True) * SCALE2
        w, added = weigh(parts, bias + [None], peak)
        acc[at] = jnp.dot(w, v[window, at[1]], preferred_element_type=jnp.float32)
        top[at] = jnp.broadcast_to(peak, (BLOCK, D))
        total[at] = jnp.broadcast_to(added, (BLOCK, D))

    def far(b, h):
        at = place(b, h)
        listed = [list_ref[b, g] for g in range(G)]
        slots = [jnp.maximum(j, 0) // per for j in listed]
        keys = jnp.concatenate([kc[h][i] for i in slots], axis=0)
        values = jnp.concatenate([vc[h][i] for i in slots], axis=0)
        parts = scores(q[at], keys)
        bias = [jnp.where(j >= 0, 0.0, NEG) for j in listed]
        peak = functools.reduce(jnp.maximum, [part + off for part, off in zip(parts, bias)])
        before = top[at]
        peak = jnp.maximum(before, jnp.max(peak, axis=1, keepdims=True) * SCALE2)
        w, added = weigh(parts, bias, peak)
        keep = jnp.exp2(before - peak)
        blend = acc[at] * keep + jnp.dot(w, values, preferred_element_type=jnp.float32)
        o[at] = (blend / (total[at] * keep + added)).astype(o.dtype)

    def give(delta, h):
        p = (me + delta) % heads
        return pltpu.make_async_remote_copy(
            src_ref=o.at[row(p, 0, rows), pl.ds(h * D, D)],
            dst_ref=out_ref.at[:, pl.ds(pl.multiple_of(me * feat + h * D, 128), D)],
            send_sem=give_send.at[h, delta],
            recv_sem=give_recv.at[h, delta],
            device_id={"head": p},
        )

    def take(delta, h):
        p = (me + heads - delta) % heads
        return pltpu.make_async_remote_copy(
            src_ref=o.at[row(p, 0, rows), pl.ds(h * D, D)],
            dst_ref=out_ref.at[:, pl.ds(pl.multiple_of(p * feat + h * D, 128), D)],
            send_sem=give_send.at[h, delta],
            recv_sem=give_recv.at[h, delta],
            device_id={"head": p},
        )

    def mine(h):
        return pltpu.make_async_copy(
            o.at[row(me, 0, rows), pl.ds(h * D, D)],
            out_ref.at[:, pl.ds(pl.multiple_of(me * feat + h * D, 128), D)],
            give_send.at[h, 0],
        )

    def blocks(s, part, h):
        at_once = math.gcd(per, 4)

        @pl.loop(0, per // at_once)
        def _(j):
            for i in range(at_once):
                part(s * per + j * at_once + i, h)

    def finish(s, delta, h):
        blocks(s, far, h)

        @pl.when(delta == 0)
        def _():
            mine(h).start()

        @pl.when(delta > 0)
        def _():
            give(delta, h).start()

    inner = rim // rows

    for h in range(hpd):
        if h > 0:
            keys_here(h)

        @pl.loop(0, heads)
        def _(delta):
            s = (me + heads - delta) % heads

            @pl.when(delta == 0)
            def _():
                own(query(h)).wait()

            @pl.when(delta > 0)
            def _():
                incoming(query(h), delta).wait_recv()

            @pl.when(s >= inner)
            def _():
                blocks(s, near, h)

            if h == 0:
                for later in range(1, hpd):

                    @pl.loop(2, ctxs - 1)
                    def _(t):
                        @pl.when((z + 1 < ctxs) & (z >= t))
                        def _():
                            forward(t, s, later)

        @pl.when(z + 1 == ctxs)
        def _():
            @pl.loop(0, ctxs - 1)
            def _(t):
                @pl.loop(0, heads)
                def _(s):
                    chain(0, t, z - 1 - t, s, h).wait_recv()
                    chain(1, t, z - 1 - t, s, h).wait_recv()

        @pl.loop(1, heads + 1)
        def _(step):
            delta = step % heads
            s = (me + delta) % heads

            @pl.when(s >= inner)
            def _():
                finish(s, delta, h)

        @pl.when(z > 0)
        def _():
            edge(0, h).wait_recv()
            edge(1, h).wait_recv()

        @pl.loop(0, inner)
        def _(s):
            blocks(s, near, h)
            finish(s, (s + heads - me) % heads, h)

    for kind in kinds:
        if rest or kind // (2 * hpd) != 1:
            sent(kind)

    @pl.when(z + 1 < ctxs)
    def _():
        for h in range(hpd):
            edge(0, h).wait_send()
            edge(1, h).wait_send()

    @pl.loop(0, ctxs - 1)
    def _(t):
        @pl.when((z + 1 < ctxs) & (z >= t))
        def _():
            @pl.loop(0, heads)
            def _(s):
                for h in range(hpd):
                    chain(0, t, z - t, s, h).wait_send()
                    chain(1, t, z - t, s, h).wait_send()

    @pl.loop(1, heads)
    def _(delta):
        for h in range(hpd):
            give(delta, h).wait_send()
            take(delta, h).wait_recv()

    for h in range(hpd):
        mine(h).wait()


def solution(mesh):
    heads, ctxs = mesh.shape["head"], mesh.shape["ctx"]

    def local(queries, key_rows, value_rows, band_blocks, global_list):
        rows, width = queries.shape
        feat = width // heads
        length = rows * heads
        rim = BAND * BLOCK
        assert rows % BLOCK == 0 and BAND % (rows // BLOCK) == 0
        bf = jnp.bfloat16
        dma = pltpu.SemaphoreType.DMA
        return pl.pallas_call(
            functools.partial(kernel, heads, ctxs, rows, feat),
            out_shape=jax.ShapeDtypeStruct((rows, width), bf),
            in_specs=[pl.BlockSpec(memory_space=pltpu.SMEM)] * 2
            + [pl.BlockSpec(memory_space=pl.ANY)] * 3,
            out_specs=pl.BlockSpec(memory_space=pl.ANY),
            scratch_shapes=[
                pltpu.VMEM((length, feat), bf),
                pltpu.VMEM((length + rim, feat), bf),
                pltpu.VMEM((length + rim, feat), bf),
                [pltpu.VMEM((ctxs * heads, BLOCK, D), bf) for _ in range(feat // D)],
                [pltpu.VMEM((ctxs * heads, BLOCK, D), bf) for _ in range(feat // D)],
                pltpu.VMEM((length, feat), bf),
                pltpu.VMEM((length, feat), jnp.float32),
                pltpu.VMEM((length, feat), jnp.float32),
                pltpu.VMEM((length, feat), jnp.float32),
                dma((5 * (feat // D), heads)),
                dma((5 * (feat // D), heads)),
                dma((feat // D, heads)),
                dma((feat // D, heads)),
                dma((2, ctxs, heads, feat // D)),
                dma((2, ctxs, heads, feat // D)),
                dma((2, feat // D)),
                dma((2, feat // D)),
                dma((2, heads, feat // D)),
            ],
            compiler_params=pltpu.CompilerParams(
                collective_id=0, has_side_effects=True, vmem_limit_bytes=48 * 1024 * 1024
            ),
        )(band_blocks, global_list, queries, key_rows, value_rows)

    in_specs = (
        P(("ctx", "head"), None),
        P(("ctx", "head"), None),
        P(("ctx", "head"), None),
        P("head"),
        P("ctx", None),
    )
    return jax.shard_map(
        local, mesh=mesh, in_specs=in_specs, out_specs=P(("ctx", "head"), None), check_vma=False
    )
```

```python
import functools
import math

import jax
import jax.numpy as jnp
from jax import lax
from jax.experimental import pallas as pl
from jax.experimental.pallas import tpu as pltpu
from jax.sharding import PartitionSpec as P

D = 128
BLOCK = 128
BAND = 4
G = 8
NEG = -1e30
SCALE2 = D ** (-0.5) * math.log2(math.e)


def kernel(
    heads, ctxs, rows, feat,
    band_ref, list_ref, q_hbm, k_hbm, v_hbm, out_ref,
    q, k, v, kc, vc, o, acc, top, total,
    send, recv, give_send, give_recv, chain_send, chain_recv, rim_send, rim_recv, fill_sem,
):
    me = lax.axis_index("head")
    z = lax.axis_index("ctx")
    per = rows // BLOCK
    rim = BAND * BLOCK
    length = heads * rows
    rest = rows - BLOCK
    hpd = feat // D

    barrier = pltpu.get_barrier_semaphore()

    @pl.loop(1, heads)
    def _(delta):
        pl.semaphore_signal(barrier, inc=1, device_id={"head": (me + delta) % heads})

    pl.semaphore_signal(barrier, inc=1, device_id={"ctx": (z + 1) % ctxs})
    pl.semaphore_signal(barrier, inc=1, device_id={"ctx": (z + ctxs - 1) % ctxs})
    pl.semaphore_wait(barrier, heads + 1)

    def col(p):
        return pl.ds(pl.multiple_of(p * feat, 128), feat)

    def row(s, first, n):
        return pl.ds(pl.multiple_of(first + s * rows, 128), n)

    def last(which, h):
        return 2 * h + which

    def before(which, h):
        return 2 * hpd + 2 * h + which

    def query(h):
        return 4 * hpd + h

    kinds = range(5 * hpd)

    def src(kind, p):
        if kind >= 4 * hpd:
            hbm, h, at = q_hbm, kind - 4 * hpd, pl.ds(0, rows)
        else:
            hbm, h = (v_hbm if kind % 2 else k_hbm), kind // 2 % hpd
            at = pl.ds(rest, BLOCK) if kind < 2 * hpd else pl.ds(0, rest)
        return hbm.at[at, pl.ds(pl.multiple_of(p * feat + h * D, 128), D)]

    def dst(kind, s):
        if kind >= 4 * hpd:
            return q.at[row(s, 0, rows), pl.ds((kind - 4 * hpd) * D, D)]
        if kind < 2 * hpd:
            return (vc if kind % 2 else kc)[kind // 2].at[z * heads + s]
        return (v if kind % 2 else k).at[row(s, rim, rest), pl.ds(kind // 2 % hpd * D, D)]

    def outgoing(kind, delta):
        return pltpu.make_async_remote_copy(
            src_ref=src(kind, (me + delta) % heads),
            dst_ref=dst(kind, me),
            send_sem=send.at[kind, delta],
            recv_sem=recv.at[kind, delta],
            device_id={"head": (me + delta) % heads},
        )

    def incoming(kind, delta):
        s = (me + heads - delta) % heads
        return pltpu.make_async_remote_copy(
            src_ref=src(kind, s),
            dst_ref=dst(kind, s),
            send_sem=send.at[kind, delta],
            recv_sem=recv.at[kind, delta],
            device_id={"head": s},
        )

    def own(kind):
        return pltpu.make_async_copy(src(kind, me), dst(kind, me), send.at[kind, 0])

    def start(kind):
        @pl.loop(1, heads)
        def _(delta):
            outgoing(kind, delta).start()

        own(kind).start()

    def arrive(kind):
        @pl.loop(1, heads)
        def _(delta):
            incoming(kind, delta).wait_recv()

        own(kind).wait()

    def sent(kind):
        @pl.loop(1, heads)
        def _(delta):
            outgoing(kind, delta).wait_send()

    def fill(which, s, h):
        big, cand = (k, kc) if which == 0 else (v, vc)
        return pltpu.make_async_copy(
            cand[h].at[z * heads + s],
            big.at[row(s, rim + rest, BLOCK), pl.ds(h * D, D)],
            fill_sem.at[which, s, h],
        )

    def chain(which, t, group, s, h):
        part = (kc if which == 0 else vc)[h].at[group * heads + s]
        return pltpu.make_async_remote_copy(
            src_ref=part,
            dst_ref=part,
            send_sem=chain_send.at[which, t, s, h],
            recv_sem=chain_recv.at[which, t, s, h],
            device_id={"ctx": (z + 1) % ctxs},
        )

    def edge(which, h):
        big = k if which == 0 else v
        hs = pl.ds(h * D, D)
        return pltpu.make_async_remote_copy(
            src_ref=big.at[pl.ds(length, rim), hs],
            dst_ref=big.at[pl.ds(0, rim), hs],
            send_sem=rim_send.at[which, h],
            recv_sem=rim_recv.at[which, h],
            device_id={"ctx": (z + 1) % ctxs},
        )

    def start_head(h):
        if rest:
            start(before(0, h))
            start(before(1, h))
        start(query(h))

    for kind in range(2 * hpd):
        start(kind)
    start_head(0)

    @pl.when(z == 0)
    def _():
        k[pl.ds(0, rim), :] = jnp.zeros((rim, feat), k.dtype)
        v[pl.ds(0, rim), :] = jnp.zeros((rim, feat), v.dtype)

    def pass_on(s, h):
        @pl.when(z + 1 < ctxs)
        def _():
            chain(0, 0, z, s, h).start()
            chain(1, 0, z, s, h).start()

        fill(0, s, h).start()
        fill(1, s, h).start()

    def forward(t, s, h):
        for which in range(2):
            chain(which, t - 1, z - t, s, h).wait_recv()
            chain(which, t, z - t, s, h).start()

    def forward_all(t, h):
        @pl.when((z + 1 < ctxs) & (z >= t))
        def _():
            @pl.loop(0, heads)
            def _(delta):
                forward(t, (me + heads - delta) % heads, h)

    for h in range(hpd):
        own(last(0, h)).wait()
        own(last(1, h)).wait()
        pass_on(me, h)

        @pl.loop(1, heads)
        def _(delta):
            incoming(last(0, h), delta).wait_recv()
            incoming(last(1, h), delta).wait_recv()
            pass_on((me + heads - delta) % heads, h)

        if h == 0:

            @pl.loop(1, ctxs - 1)
            def _(t):
                forward_all(t, 0)

    @pl.loop(0, heads)
    def _(s):
        for h in range(hpd):
            fill(0, s, h).wait()
            fill(1, s, h).wait()

    def keys_here(h):
        if rest:
            arrive(before(0, h))
        if h + 1 < hpd:
            start_head(h + 1)
        if rest:
            arrive(before(1, h))

        @pl.when(z + 1 < ctxs)
        def _():
            edge(0, h).start()
            edge(1, h).start()

    keys_here(0)
    for h in range(1, hpd):
        forward_all(1, h)

    tri = lax.broadcasted_iota(jnp.int32, (BLOCK, BLOCK), 1) <= lax.broadcasted_iota(
        jnp.int32, (BLOCK, BLOCK), 0
    )
    first = z * (length // BLOCK)

    def weigh(parts, bias, peak):
        weights = []
        for part, off in zip(parts, bias):
            shift = peak if off is None else peak - off
            weights.append(jnp.exp2(part * SCALE2 - shift))
        added = jnp.sum(functools.reduce(jnp.add, weights), axis=1, keepdims=True)
        return jnp.concatenate([x.astype(jnp.bfloat16) for x in weights], axis=1), added

    def scores(qb, keys):
        s = lax.dot_general(
            qb, keys, (((1,), (1,)), ((), ())), preferred_element_type=jnp.float32
        )
        return [s[:, i : i + BLOCK] for i in range(0, s.shape[1], BLOCK)]

    def place(b, h):
        return pl.ds(pl.multiple_of(b * BLOCK, 128), BLOCK), pl.ds(h * D, D)

    def near(b, h):
        at = place(b, h)
        window = pl.ds(pl.multiple_of(b * BLOCK, 128), (BAND + 1) * BLOCK)
        parts = scores(q[at], k[window, at[1]])
        parts[BAND] = jnp.where(tri, parts[BAND], NEG)
        reach = band_ref[h]
        bias = [
            jnp.where((reach >= BAND - i) & (first + b >= BAND - i), 0.0, NEG) for i in range(BAND)
        ]
        peak = parts[BAND]
        for part, off in zip(parts, bias):
            peak = jnp.maximum(peak, part + off)
        peak = jnp.max(peak, axis=1, keepdims=True) * SCALE2
        w, added = weigh(parts, bias + [None], peak)
        acc[at] = jnp.dot(w, v[window, at[1]], preferred_element_type=jnp.float32)
        top[at] = jnp.broadcast_to(peak, (BLOCK, D))
        total[at] = jnp.broadcast_to(added, (BLOCK, D))

    def far(b, h):
        at = place(b, h)
        listed = [list_ref[b, g] for g in range(G)]
        slots = [jnp.maximum(j, 0) // per for j in listed]
        keys = jnp.concatenate([kc[h][i] for i in slots], axis=0)
        values = jnp.concatenate([vc[h][i] for i in slots], axis=0)
        parts = scores(q[at], keys)
        bias = [jnp.where(j >= 0, 0.0, NEG) for j in listed]
        peak = functools.reduce(jnp.maximum, [part + off for part, off in zip(parts, bias)])
        before = top[at]
        peak = jnp.maximum(before, jnp.max(peak, axis=1, keepdims=True) * SCALE2)
        w, added = weigh(parts, bias, peak)
        keep = jnp.exp2(before - peak)
        blend = acc[at] * keep + jnp.dot(w, values, preferred_element_type=jnp.float32)
        o[at] = (blend / (total[at] * keep + added)).astype(o.dtype)

    def give(delta, h):
        p = (me + delta) % heads
        return pltpu.make_async_remote_copy(
            src_ref=o.at[row(p, 0, rows), pl.ds(h * D, D)],
            dst_ref=out_ref.at[:, pl.ds(pl.multiple_of(me * feat + h * D, 128), D)],
            send_sem=give_send.at[h, delta],
            recv_sem=give_recv.at[h, delta],
            device_id={"head": p},
        )

    def take(delta, h):
        p = (me + heads - delta) % heads
        return pltpu.make_async_remote_copy(
            src_ref=o.at[row(p, 0, rows), pl.ds(h * D, D)],
            dst_ref=out_ref.at[:, pl.ds(pl.multiple_of(p * feat + h * D, 128), D)],
            send_sem=give_send.at[h, delta],
            recv_sem=give_recv.at[h, delta],
            device_id={"head": p},
        )

    def mine(h):
        return pltpu.make_async_copy(
            o.at[row(me, 0, rows), pl.ds(h * D, D)],
            out_ref.at[:, pl.ds(pl.multiple_of(me * feat + h * D, 128), D)],
            give_send.at[h, 0],
        )

    def blocks(s, part, h):
        at_once = math.gcd(per, 4)

        @pl.loop(0, per // at_once)
        def _(j):
            for i in range(at_once):
                part(s * per + j * at_once + i, h)

    def finish(s, delta, h):
        blocks(s, far, h)

        @pl.when(delta == 0)
        def _():
            mine(h).start()

        @pl.when(delta > 0)
        def _():
            give(delta, h).start()

    inner = rim // rows

    for h in range(hpd):
        if h > 0:
            keys_here(h)

        @pl.loop(0, heads)
        def _(delta):
            s = (me + heads - delta) % heads

            @pl.when(delta == 0)
            def _():
                own(query(h)).wait()

            @pl.when(delta > 0)
            def _():
                incoming(query(h), delta).wait_recv()

            @pl.when(s >= inner)
            def _():
                blocks(s, near, h)

            if h == 0:
                for later in range(1, hpd):

                    @pl.loop(2, ctxs - 1)
                    def _(t):
                        @pl.when((z + 1 < ctxs) & (z >= t))
                        def _():
                            forward(t, s, later)

        @pl.when(z + 1 == ctxs)
        def _():
            @pl.loop(0, ctxs - 1)
            def _(t):
                @pl.loop(0, heads)
                def _(s):
                    chain(0, t, z - 1 - t, s, h).wait_recv()
                    chain(1, t, z - 1 - t, s, h).wait_recv()

        @pl.loop(1, heads + 1)
        def _(step):
            delta = step % heads
            s = (me + delta) % heads

            @pl.when(s >= inner)
            def _():
                finish(s, delta, h)

        @pl.when(z > 0)
        def _():
            edge(0, h).wait_recv()
            edge(1, h).wait_recv()

        @pl.loop(0, inner)
        def _(s):
            blocks(s, near, h)
            finish(s, (s + heads - me) % heads, h)

    for kind in kinds:
        if rest or kind // (2 * hpd) != 1:
            sent(kind)

    @pl.when(z + 1 < ctxs)
    def _():
        for h in range(hpd):
            edge(0, h).wait_send()
            edge(1, h).wait_send()

    @pl.loop(0, ctxs - 1)
    def _(t):
        @pl.when((z + 1 < ctxs) & (z >= t))
        def _():
            @pl.loop(0, heads)
            def _(s):
                for h in range(hpd):
                    chain(0, t, z - t, s, h).wait_send()
                    chain(1, t, z - t, s, h).wait_send()

    @pl.loop(1, heads)
    def _(delta):
        for h in range(hpd):
            give(delta, h).wait_send()
            take(delta, h).wait_recv()

    for h in range(hpd):
        mine(h).wait()


def solution(mesh):
    heads, ctxs = mesh.shape["head"], mesh.shape["ctx"]

    def local(queries, key_rows, value_rows, band_blocks, global_list):
        rows, width = queries.shape
        feat = width // heads
        length = rows * heads
        rim = BAND * BLOCK
        assert rows % BLOCK == 0 and BAND % (rows // BLOCK) == 0
        bf = jnp.bfloat16
        dma = pltpu.SemaphoreType.DMA
        return pl.pallas_call(
            functools.partial(kernel, heads, ctxs, rows, feat),
            out_shape=jax.ShapeDtypeStruct((rows, width), bf),
            in_specs=[pl.BlockSpec(memory_space=pltpu.SMEM)] * 2
            + [pl.BlockSpec(memory_space=pl.ANY)] * 3,
            out_specs=pl.BlockSpec(memory_space=pl.ANY),
            scratch_shapes=[
                pltpu.VMEM((length, feat), bf),
                pltpu.VMEM((length + rim, feat), bf),
                pltpu.VMEM((length + rim, feat), bf),
                [pltpu.VMEM((ctxs * heads, BLOCK, D), bf) for _ in range(feat // D)],
                [pltpu.VMEM((ctxs * heads, BLOCK, D), bf) for _ in range(feat // D)],
                pltpu.VMEM((length, feat), bf),
                pltpu.VMEM((length, feat), jnp.float32),
                pltpu.VMEM((length, feat), jnp.float32),
                pltpu.VMEM((length, feat), jnp.float32),
                dma((5 * (feat // D), heads)),
                dma((5 * (feat // D), heads)),
                dma((feat // D, heads)),
                dma((feat // D, heads)),
                dma((2, ctxs, heads, feat // D)),
                dma((2, ctxs, heads, feat // D)),
                dma((2, feat // D)),
                dma((2, feat // D)),
                dma((2, heads, feat // D)),
            ],
            compiler_params=pltpu.CompilerParams(
                collective_id=0, has_side_effects=True, vmem_limit_bytes=48 * 1024 * 1024
            ),
        )(band_blocks, global_list, queries, key_rows, value_rows)

    in_specs = (
        P(("ctx", "head"), None),
        P(("ctx", "head"), None),
        P(("ctx", "head"), None),
        P("head"),
        P("ctx", None),
    )
    return jax.shard_map(
        local, mesh=mesh, in_specs=in_specs, out_specs=P(("ctx", "head"), None), check_vma=False
    )
```
